512 devices in a mesh: member: 64 (over z, x), region: 8 (over y, core).
Axes of the slice: x: 4, y: 4, z: 16, core: 2. Of those that a mesh axis runs over, the one named last changes fastest.
Arguments:
- states: bfloat16 [512, 1024, 768], P('member', 'region'), may hold values from -6 to 6
- observed: bfloat16 [512, 1024, 256], P('member', 'region'), may hold values from -6 to 6
- precision: float32 [1024, 256], P('region'), may hold values from 0.3 to 4
- innovation: float32 [1024, 256], P('region'), may hold values from -6 to 6
- obs_column: int32 [1024, 256], P('region'), may hold values from 0 to 63
- nearby: int32 [1024, 3], P('region'), may hold values from 0 to 1023, as said below
Outputs:
- analysis: bfloat16 [512, 1024, 768], P('member', 'region')
The draws below stay inside these ranges and needn't reach their ends.
Inputs may be any that keep to these rules, and one draw needn't show every extreme that they name: `nearby`: row b lists 3 different observation blocks: b itself first, then blocks at cycle distance at most 4 from b (blocks 0 and 1024 - 1 are neighbours), one at distance exactly 4.
All inputs are finite; a program needn't handle non-finite values. Where the reference program divides by a largest or mean magnitude, that divisor is 1e-20 or more.
Results may differ from the reference program's by a relative error of at most 0.0043.
The reference program's roundings to bfloat16 on the way count: a program that leaves them out, or rounds other values in their place, can miss the bound.
Values may be sent and summed in bfloat16 or wider, within the bound.
A program may use at most 64 MiB of HBM per device.

```python
import math
import jax
import jax.numpy as jnp
from jax import lax

K = 512
COLS = 64
OBS = 256
RADIUS = 4
NEAR = 3
NS_STEPS = 3
NBLK = 1024
SITES = 768


def draw_nearby(key, part):
    key = jax.random.fold_in(key, 7)
    key_pick, key_side = jax.random.split(key)
    candidates = jnp.concatenate([jnp.arange(1, RADIUS), -jnp.arange(1, RADIUS)]).astype(jnp.int32)
    row_keys = jax.random.split(key_pick, NBLK)

    def shuffled(row_key):
        return jax.random.permutation(row_key, candidates)
    picked = jax.vmap(shuffled)(row_keys)[:, :NEAR - 2]
    side_sign = jax.random.randint(key_side, (NBLK, 1), 0, 2).astype(jnp.int32) * 2 - 1
    offsets = jnp.concatenate([jnp.zeros((NBLK, 1), jnp.int32), side_sign * RADIUS, picked], axis=1)
    block_ids = jnp.arange(NBLK, dtype=jnp.int32)[:, None]
    return jnp.mod(block_ids + offsets, NBLK).astype(jnp.int32)


def set_ends(drawn, key, low, largest):
    longest = drawn.shape.index(max(drawn.shape))
    spots = []
    for shift in (0, 1):
        where = [jax.random.randint(jax.random.fold_in(key, axis), (), 0, length) for axis, length in enumerate(drawn.shape)]
        where[longest] = (where[longest] + shift) % drawn.shape[longest]
        spots.append(tuple(where))
    return drawn.at[spots[0]].set(low).at[spots[1]].set(largest)


def level_of(key, extent, cuts, low, largest):
    level, own = 1.0, jax.random.fold_in(key, 6)
    for axis_at, blocks in cuts:
        steps = jnp.exp(jax.random.uniform(jax.random.fold_in(own, axis_at), (blocks,), jnp.float32, low / len(cuts), largest / len(cuts)))
        level = level * jnp.repeat(steps, extent[axis_at] // blocks).reshape([-1 if axis == axis_at else 1 for axis in range(len(extent))])
    return level


def scatter_about(key, extent, scale, bound, pieces=(), held_as=jnp.bfloat16):
    result = jax.random.normal(key, extent, jnp.float32) * scale
    if len(pieces) > 0:
        result = level_of(key, extent, pieces, -0.22, 0.18) * result
    return jnp.clip(result, min=-bound, max=bound).astype(held_as)


def setup_inputs(seed: int = 0) -> dict:
    key_of = jax.random.split(jax.random.key(seed), 7)
    states = scatter_about(key_of[0], (K, NBLK, SITES), 1.0, 6.0, ((0, 64), (1, 8)))
    observed = scatter_about(key_of[1], (K, NBLK, OBS), 1.0, 6.0, ((0, 64), (1, 8)))
    precision = jnp.clip(jnp.exp(math.log(4.0) - 2.5902671 * jax.random.uniform(key_of[2], (NBLK, OBS), jnp.float32) ** level_of(key_of[2], (NBLK, OBS), ((0, 8),), -0.2, 0.2)), 0.3, 4.0)
    innovation = scatter_about(key_of[3], (NBLK, OBS), 1.0, 6.0, ((0, 8),), jnp.float32)
    obs_column = set_ends(jax.random.randint(key_of[4], (NBLK, OBS), 0, COLS), jax.random.fold_in(key_of[4], 1), 0, COLS - 1).astype(jnp.int32)
    nearby = draw_nearby(jax.random.fold_in(key_of[6], 71), 0)
    return dict(states=states, observed=observed, precision=precision, innovation=innovation, obs_column=obs_column, nearby=nearby)


def highest(left, right):
    return jnp.dot(left, right, precision=lax.Precision.HIGHEST)

def transform(members, obs_rows, obs_precision, obs_innovation, obs_columns, offsets):
    ensemble = members.shape[0]
    member_float = members.astype(jnp.float32)
    mean_state = lax.optimization_barrier(jnp.mean(member_float, axis=0))
    state_pert = (member_float - mean_state).astype(jnp.bfloat16)
    obs_float = obs_rows.astype(jnp.float32)
    obs_pert = (obs_float - lax.optimization_barrier(jnp.mean(obs_float, axis=0))).astype(jnp.bfloat16)
    distance = COLS * offsets + obs_columns - 0.5 * (COLS - 1)
    local_weight = obs_precision * jnp.exp(-0.5 * jnp.square(distance / (0.5 * COLS * RADIUS)))
    weighted = (obs_pert.astype(jnp.float32) * local_weight).astype(jnp.bfloat16)
    product = lax.dot_general(weighted, obs_pert, (((1,), (1,)), ((), ())), preferred_element_type=jnp.float32)
    forcing = highest(weighted.astype(jnp.float32), obs_innovation)
    identity = jnp.eye(ensemble, dtype=jnp.float32)
    system = product + (ensemble - 1.0) * identity
    row_bound = jnp.max(lax.optimization_barrier(jnp.sum(jnp.abs(system), axis=1)))
    root_iterate = system / row_bound
    inverse_root = identity
    for iteration in range(NS_STEPS):
        if iteration == 0:
            factor = 1.5 * identity - 0.5 * root_iterate
        else:
            factor = 1.5 * identity - 0.5 * highest(inverse_root, root_iterate)
        if iteration < NS_STEPS - 1:
            root_iterate = highest(root_iterate, factor)
        inverse_root = factor if iteration == 0 else highest(factor, inverse_root)
    mean_weight = highest(inverse_root, highest(inverse_root, forcing)) / row_bound
    weights = (jnp.sqrt((ensemble - 1.0) / row_bound) * inverse_root + mean_weight[:, None]).astype(jnp.bfloat16)
    analysed = lax.dot_general(weights, state_pert, (((0,), (0,)), ((), ())), preferred_element_type=jnp.float32)
    return (mean_state + analysed).astype(jnp.bfloat16)

def reference(states, observed, precision, innovation, obs_column, nearby):
    total_blocks = states.shape[1]
    ensemble = states.shape[0]

    def one_block(block_index):
        near_ids = nearby[block_index]
        offsets = (jnp.mod(near_ids - block_index + total_blocks // 2, total_blocks) - total_blocks // 2).astype(jnp.float32)
        members = lax.dynamic_index_in_dim(states, block_index, 1, keepdims=False)
        obs_rows = jnp.take(observed, near_ids, axis=1).reshape(ensemble, -1)
        obs_precision = jnp.take(precision, near_ids, axis=0).reshape(-1)
        obs_innovation = jnp.take(innovation, near_ids, axis=0).reshape(-1)
        obs_columns = jnp.take(obs_column, near_ids, axis=0).reshape(-1).astype(jnp.float32)
        return transform(members, obs_rows, obs_precision, obs_innovation, obs_columns, jnp.repeat(offsets, OBS))
    blocks = lax.map(one_block, jnp.arange(total_blocks, dtype=jnp.int32))
    return jnp.transpose(blocks, (1, 0, 2))
```

```python
import jax
import jax.numpy as jnp
from jax import lax
from jax.experimental import pallas as pl
from jax.experimental.pallas import tpu as pltpu
from jax.sharding import PartitionSpec as P

MESH = pl.DeviceIdType.MESH
F32 = jnp.float32
BF16 = jnp.bfloat16

COLS = 64
RADIUS = 4
NZ, NX, NY = 16, 4, 4
K = 512
OBS = 256
SITES = 768
WINDOW = 10
PIECES = 3
WIDTH = SITES // PIECES
HALF = K // 2


def dot_nn(a, b):
    return jnp.dot(a, b, preferred_element_type=F32)


def dot_nt(a, b):
    return lax.dot_general(a, b, (((1,), (1,)), ((), ())), preferred_element_type=F32)


def split_rows(v):
    high = v.astype(BF16).astype(F32)
    rest = v - high
    mid = rest.astype(BF16).astype(F32)
    low = rest - mid
    row = lax.broadcasted_iota(jnp.int32, (16, v.shape[1]), 0)
    zero = jnp.zeros((16, v.shape[1]), F32)
    stacked = jnp.where(row == 0, high, jnp.where(row == 1, mid, jnp.where(row == 2, low, zero)))
    return stacked.astype(BF16)


def as_row(v):
    return jnp.concatenate([v[0:1], v[1:2]], axis=1)


def identity_rows(start, scale):
    row = lax.broadcasted_iota(jnp.int32, (HALF, K), 0) + start
    col = lax.broadcasted_iota(jnp.int32, (HALF, K), 1)
    return jnp.where(row == col, F32(scale), F32(0.0))


def kernel(
    states, obs, meta, out,
    own_obs, window, arrived, results, meta_win, pert, weighted, innov, high, low, full, trans,
    meta_send, meta_recv, obs_send, obs_recv, win_send, win_recv, st_send, st_recv, out_send, out_recv,
):
    member = lax.axis_index("member")
    region = lax.axis_index("region")
    z, x = lax.div(member, NX), lax.rem(member, NX)
    y, c = lax.div(region, 2), lax.rem(region, 2)
    half, inner = lax.div(z, 8), lax.rem(z, 8)
    place = 2 * x + c
    z_next, z_prev = lax.rem(z + 1, NZ), lax.rem(z + NZ - 1, NZ)
    y_next = lax.rem(y + lax.div(z + 1, NZ), NY)
    y_prev = lax.rem(y + NY - 1 + lax.div(z + NZ - 1, NZ), NY)
    holder = c == half

    def device(zz, xx, yy, cc):
        return (zz * NX + xx, yy * 2 + cc)

    def remote(src, dst, send, recv, target):
        pltpu.make_async_remote_copy(
            src_ref=src, dst_ref=dst, send_sem=send, recv_sem=recv, device_id=target, device_id_type=MESH
        ).start()

    def local(src, dst, sem):
        pltpu.make_async_copy(src, dst, sem).start()

    def drain(ref, sem):
        pltpu.make_async_copy(ref, ref, sem).wait()

    def slot_of(zz, xx):
        return xx * 16 + lax.rem(zz, 2) * 8 + lax.div(zz, 2)

    barrier = pltpu.get_barrier_semaphore()

    def greet(t, carry):
        target = device(
            lax.rem(z + lax.div(t, 8), NZ), lax.rem(x + lax.rem(lax.div(t, 2), NX), NX), y, lax.rem(c + t, 2)
        )
        pl.semaphore_signal(barrier, inc=1, device_id=target, device_id_type=MESH)
        return carry

    lax.fori_loop(1, NZ * NX * 2, greet, 0)
    edge = (z == 0) | (z == NZ - 1)

    @pl.when(edge)
    def _():
        zz = NZ - 1 - z
        yy = lax.select(z == 0, y_prev, y_next)
        for j in range(8):
            pl.semaphore_signal(barrier, inc=1, device_id=device(zz, j // 2, yy, j % 2), device_id_type=MESH)

    pl.semaphore_wait(barrier, NZ * NX * 2 - 1 + 8 * edge.astype(jnp.int32))

    parity = lax.rem(z, 2)

    def send_obs(t, carry):
        ii = lax.rem(inner + t, 8)
        zz = 8 * c + ii
        src = obs.at[pl.ds(pl.multiple_of(ii * 128, 128), 128)]
        dst = own_obs.at[lax.div(z, 2)]
        mine = (zz == z) & (parity == c)

        @pl.when(mine)
        def _():
            local(src, dst, obs_recv)

        @pl.when(jnp.logical_not(mine))
        def _():
            remote(src, dst, obs_send, obs_recv, device(zz, x, y, parity))

        return carry

    lax.fori_loop(0, 8, send_obs, 0)

    @pl.when(holder)
    def _():
        start = inner * 16
        own = meta.at[pl.ds(start, 16)]
        local(own, meta_win.at[pl.ds(8, 16)], meta_recv)
        remote(own, meta_win.at[pl.ds(8, 16)], meta_send, meta_recv, device(z, x, y, 1 - c))
        for cc in range(2):
            remote(meta.at[pl.ds(start, 8)], meta_win.at[pl.ds(24, 8)], meta_send, meta_recv,
                   device(z_prev, x, y_prev, cc))
            remote(meta.at[pl.ds(start + 8, 8)], meta_win.at[pl.ds(0, 8)], meta_send, meta_recv,
                   device(z_next, x, y_next, cc))

    def send_states(piece):
        cols = pl.ds(piece * WIDTH, WIDTH)

        def body(t, carry):
            ii = lax.rem(inner + lax.div(t, 8), 8)
            zz = 8 * c + ii
            xx = lax.rem(x + lax.rem(lax.div(t, 2), NX), NX)
            cc = lax.rem(c + t, 2)
            src = states.at[ii * 8 + 2 * xx + cc, :, cols]
            dst = arrived.at[slot_of(z, x), :, cols]
            mine = (zz == z) & (xx == x) & (cc == c)

            @pl.when(mine)
            def _():
                local(src, dst, st_recv.at[piece])

            @pl.when(jnp.logical_not(mine))
            def _():
                remote(src, dst, st_send, st_recv.at[piece], device(zz, xx, y, cc))

            return carry

        lax.fori_loop(0, 64, body, 0)

    self_obs = holder & (parity == c)

    @pl.when(self_obs)
    def _():
        drain(own_obs.at[pl.ds(0, 7)], obs_send)

    @pl.when(jnp.logical_not(self_obs))
    def _():
        drain(own_obs, obs_send)

    send_states(0)
    drain(own_obs, obs_recv)

    mine_at = pl.ds(pl.multiple_of(place * 8, 8), 8)
    for step in range(8):
        for q in range(8):
            first, last = max(0, 2 * q - 4), min(16, 2 * q + 6)
            src = own_obs.at[:, pl.ds(first * 8, (last - first) * 8)]
            dst = window.at[mine_at, pl.ds((first - 2 * q + 4) * 8, (last - first) * 8)]
            if step > 0:

                @pl.when(lax.rem(place + step, 8) == q)
                def _():
                    remote(src, dst, win_send, win_recv, device(z, q // 2, y, q % 2))

            else:

                @pl.when(place == q)
                def _():
                    local(src, dst, win_recv)

    for q, rows in ((0, 4), (1, 2)):
        remote(own_obs.at[:, pl.ds((16 - rows) * 8, rows * 8)], window.at[mine_at, pl.ds(0, rows * 8)],
               win_send, win_recv, device(z_next, q // 2, y_next, q % 2))
    for q, rows in ((7, 4), (6, 2)):
        remote(own_obs.at[:, pl.ds(0, rows * 8)], window.at[mine_at, pl.ds((WINDOW - rows) * 8, rows * 8)],
               win_send, win_recv, device(z_prev, q // 2, y_prev, q % 2))

    for piece in range(1, PIECES):
        send_states(piece)

    drain(meta_win, meta_recv)
    listed = [meta_win[8 + 2 * place + b][6:7] for b in range(2)]
    local_weight = [[None] * WINDOW for _ in range(2)]
    for w in range(WINDOW):
        row = meta_win[2 * place + 4 + w]
        precision, column = row[0:2], row[4:6]
        innov[:, w * OBS : (w + 1) * OBS] = split_rows(as_row(row[2:4]))
        for b in range(2):
            if 0 <= w - b <= 2 * RADIUS:
                distance = F32(COLS * (w - b - RADIUS)) + column - F32(0.5 * (COLS - 1))
                decay = jnp.exp(-0.5 * jnp.square(distance / (0.5 * COLS * RADIUS)))
                local_weight[b][w] = as_row(precision * decay * listed[b][:, w - b : w - b + 1])

    drain(window, win_recv)
    for pair in range(WINDOW // 2):
        rows = window[:, pair * 16 : (pair + 1) * 16, :].astype(F32)
        for e in range(2):
            w = 2 * pair + e
            at = slice(w * OBS, (w + 1) * OBS)
            values = rows[:, 8 * e : 8 * e + 8, :].reshape(K, OBS)
            anomaly = (values - jnp.mean(values, axis=0, keepdims=True)).astype(BF16)
            pert[:, at] = anomaly
            anomaly = anomaly.astype(F32)
            for b in range(2):
                if local_weight[b][w] is not None:
                    weighted[b, :, at] = (anomaly * local_weight[b][w]).astype(BF16)

    def put(k, rows, value):
        top = value.astype(BF16)
        high[k, rows, :] = top
        low[k, rows, :] = (value - top.astype(F32)).astype(BF16)

    def product(a, b, rows):
        left = high[a, rows, :]
        return dot_nn(left, high[b]) + dot_nn(left, low[b]) + dot_nn(low[a, rows, :], high[b])

    def halves(step):
        @pl.loop(0, 2)
        def _(t):
            start = pl.multiple_of(t * HALF, HALF)
            step(pl.ds(start, HALF), start)

    def times(v, k):
        parts = split_rows(v)
        return jnp.sum(dot_nn(parts, high[k]) + dot_nn(parts, low[k]), axis=0, keepdims=True)

    R, F0, R1, F1, R2, Z2, F2, Z3 = range(8)

    @pl.loop(0, 2)
    def _(b):
        span = pl.ds(pl.multiple_of(b * OBS, OBS), (2 * RADIUS + 1) * OBS)

        def system(rows, start):
            full[rows, :] = dot_nt(pert[rows, span], weighted[b, :, span]) + identity_rows(start, K - 1.0)

        halves(system)
        row_bound = jnp.max(jnp.sum(jnp.abs(full[...]), axis=0, keepdims=True), axis=1, keepdims=True)
        inverse = 1.0 / row_bound

        def first(rows, start):
            value = full[rows, :] * inverse
            put(R, rows, value)
            put(F0, rows, identity_rows(start, 1.5) - 0.5 * value)

        def second(rows, start):
            put(R1, rows, product(R, F0, rows))

        def third(rows, start):
            put(F1, rows, identity_rows(start, 1.5) - 0.5 * product(F0, R1, rows))

        def fourth(rows, start):
            put(R2, rows, product(R1, F1, rows))
            put(Z2, rows, product(F1, F0, rows))

        def fifth(rows, start):
            put(F2, rows, identity_rows(start, 1.5) - 0.5 * product(Z2, R2, rows))

        def sixth(rows, start):
            value = product(F2, Z2, rows)
            full[rows, :] = value
            put(Z3, rows, value)

        for step in (first, second, third, fourth, fifth, sixth):
            halves(step)

        forcing = jnp.sum(dot_nt(innov[:, span], weighted[b, :, span]), axis=0, keepdims=True)
        mean_weight = times(times(forcing, Z3), Z3) * inverse
        scale = jnp.sqrt((K - 1.0) * inverse)

        def weights(rows, start):
            trans[b, rows, :] = (scale * full[rows, :] + mean_weight).astype(BF16)

        halves(weights)

    for piece in range(PIECES):
        cols = pl.ds(piece * WIDTH, WIDTH)
        drain(arrived.at[:, :, cols], st_recv.at[piece])
        chunk = arrived[:, :, piece * WIDTH : (piece + 1) * WIDTH].astype(F32)
        blocks = []
        for b in range(2):
            values = chunk[:, 8 * b : 8 * b + 8, :].reshape(K, WIDTH)
            mean = jnp.mean(values, axis=0, keepdims=True)
            analysed = mean + dot_nn(trans[b], (values - mean).astype(BF16))
            blocks.append(analysed.reshape(64, 8, WIDTH))
        results[:, :, piece * WIDTH : (piece + 1) * WIDTH] = jnp.concatenate(blocks, axis=1).astype(BF16)

        def give_back(t, carry):
            zz = lax.rem(z + lax.div(t, NX), NZ)
            xx = lax.rem(x + t, NX)
            src = results.at[slot_of(zz, xx), :, cols]
            dst = out.at[inner * 8 + place, :, cols]
            mine = (zz == z) & (xx == x) & holder

            @pl.when(mine)
            def _():
                local(src, dst, out_recv)

            @pl.when(jnp.logical_not(mine))
            def _():
                remote(src, dst, out_send, out_recv, device(zz, xx, y, half))

            return carry

        lax.fori_loop(0, 64, give_back, 0)

    drain(out, out_recv)

    @pl.when(holder)
    def _():
        drain(meta.at[pl.ds(0, 48)], meta_send)
        drain(states.at[pl.ds(0, 63)], st_send)
        drain(results.at[pl.ds(0, 63)], out_send)

    @pl.when(jnp.logical_not(holder))
    def _():
        drain(states, st_send)
        drain(results, out_send)

    for q in range(8):
        kept = min(16, 2 * q + 6) - max(0, 2 * q - 4)

        @pl.when(place == q)
        def _():
            drain(own_obs.at[:, pl.ds(0, (16 - kept) * 8)], win_send)

    for _ in range(4):
        drain(own_obs, win_send)


def on_device(states, observed, precision, innovation, obs_column, nearby):
    local_blocks = states.shape[1]
    total_blocks = local_blocks * lax.axis_size("region")
    block_ids = lax.axis_index("region") * local_blocks + jnp.arange(local_blocks, dtype=jnp.int32)
    offsets = (
        jnp.mod(nearby - block_ids[:, None] + total_blocks // 2, total_blocks) - total_blocks // 2
    )
    lanes = jnp.arange(128, dtype=jnp.int32) - RADIUS
    listed = jnp.any(offsets[:, :, None] == lanes[None, None, :], axis=1).astype(F32)
    meta = jnp.concatenate(
        [precision, innovation, obs_column.astype(F32), listed, jnp.zeros_like(listed)], axis=1
    ).reshape(local_blocks, 8, 128)
    chunks = states.reshape(8, 64, 2, SITES).transpose(1, 2, 0, 3).reshape(64, 16, SITES)
    obs_rows = observed.transpose(1, 0, 2).reshape(local_blocks * 8, OBS)

    vmem = pl.BlockSpec(memory_space=pltpu.VMEM)
    dma = pltpu.SemaphoreType.DMA
    gathered = pl.pallas_call(
        kernel,
        out_shape=jax.ShapeDtypeStruct((64, 16, SITES), BF16),
        in_specs=[vmem] * 3,
        out_specs=vmem,
        scratch_shapes=[
            pltpu.VMEM((8, 128, OBS), BF16),
            pltpu.VMEM((64, 8 * WINDOW, OBS), BF16),
            pltpu.VMEM((64, 16, SITES), BF16),
            pltpu.VMEM((64, 16, SITES), BF16),
            pltpu.VMEM((32, 8, 128), F32),
            pltpu.VMEM((K, WINDOW * OBS), BF16),
            pltpu.VMEM((2, K, WINDOW * OBS), BF16),
            pltpu.VMEM((16, WINDOW * OBS), BF16),
            pltpu.VMEM((8, K, K), BF16),
            pltpu.VMEM((8, K, K), BF16),
            pltpu.VMEM((K, K), F32),
            pltpu.VMEM((2, K, K), BF16),
            dma, dma, dma, dma, dma, dma, dma, dma((PIECES,)), dma, dma,
        ],
        compiler_params=pltpu.CompilerParams(
            collective_id=0, has_side_effects=True, vmem_limit_bytes=48 * 1024 * 1024
        ),
    )(chunks, obs_rows, meta)
    return gathered.reshape(64, 2, 8, SITES).transpose(2, 0, 1, 3).reshape(8, local_blocks, SITES)


def solution(mesh):
    split = P("region", None)
    placed = (P("member", "region", None), P("member", "region", None), split, split, split, split)
    return jax.shard_map(
        on_device, mesh=mesh, in_specs=placed, out_specs=P("member", "region", None), check_vma=False
    )
```

```python
import jax
import jax.numpy as jnp
from jax import lax
from jax.experimental import pallas as pl
from jax.experimental.pallas import tpu as pltpu
from jax.sharding import PartitionSpec as P

MESH = pl.DeviceIdType.MESH
F32 = jnp.float32
BF16 = jnp.bfloat16

COLS = 64
RADIUS = 4
NBLK = 1024
NZ, NX, NY = 16, 4, 4
K = 512
OBS = 256
SITES = 768
PAIRS = 5
PIECES = 3
WIDTH = SITES // PIECES
TILE = 256


def dot_nn(a, b):
    return jnp.dot(a, b, preferred_element_type=F32)


def dot_nt(a, b):
    return lax.dot_general(a, b, (((1,), (1,)), ((), ())), preferred_element_type=F32)


def split_rows(v):
    top = v.astype(BF16).astype(F32)
    rest = v - top
    mid = rest.astype(BF16).astype(F32)
    row = lax.broadcasted_iota(jnp.int32, (16, v.shape[1]), 0)
    zero = jnp.zeros((16, v.shape[1]), F32)
    stacked = jnp.where(row == 0, top, jnp.where(row == 1, mid, jnp.where(row == 2, rest - mid, zero)))
    return stacked.astype(BF16)


def as_row(v):
    return jnp.concatenate([v[0:1], v[1:2]], axis=1)


def identity_rows(start, scale):
    row = lax.broadcasted_iota(jnp.int32, (TILE, K), 0) + start
    col = lax.broadcasted_iota(jnp.int32, (TILE, K), 1)
    return jnp.where(row == col, F32(scale), F32(0.0))


def kernel(
    states_hbm, observed_hbm, precision_hbm, innovation_hbm, column_hbm, nearby_hbm, out,
    states, observed, precision, innovation, column, nearby, load_sem,
    wide, chunks, obs, meta, own_obs, window, arrived, results, meta_win, weighted, high, low, full, trans,
    meta_send, meta_recv, obs_send, obs_recv, win_send, win_recv, st_send, st_recv, out_send, out_recv,
    row_ready,
):
    member = lax.axis_index("member")
    region = lax.axis_index("region")
    z, x = lax.div(member, NX), lax.rem(member, NX)
    y, c = lax.div(region, 2), lax.rem(region, 2)
    half, inner = lax.div(z, 8), lax.rem(z, 8)
    place = 2 * x + c
    parity = lax.rem(z, 2)
    z_next, z_prev = lax.rem(z + 1, NZ), lax.rem(z + NZ - 1, NZ)
    y_next = lax.rem(y + lax.div(z + 1, NZ), NY)
    y_prev = lax.rem(y + NY - 1 + lax.div(z + NZ - 1, NZ), NY)
    holder = c == half

    def device(zz, xx, yy, cc):
        return (zz * NX + xx, yy * 2 + cc)

    def remote(src, dst, send, recv, target):
        pltpu.make_async_remote_copy(
            src_ref=src, dst_ref=dst, send_sem=send, recv_sem=recv, device_id=target, device_id_type=MESH
        ).start()

    def pass_on(src, dst, send, recv, target, mine):
        @pl.when(mine)
        def _():
            pltpu.make_async_copy(src, dst, recv).start()

        @pl.when(jnp.logical_not(mine))
        def _():
            remote(src, dst, send, recv, target)

    def drain(ref, sem):
        pltpu.make_async_copy(ref, ref, sem).wait()

    def slot_of(zz, xx):
        return xx * 16 + lax.rem(zz, 2) * 8 + lax.div(zz, 2)

    loads = [
        pltpu.make_async_copy(source, target, load_sem.at[k])
        for k, (source, target) in enumerate((
            (observed_hbm, observed), (states_hbm, states), (precision_hbm, precision),
            (innovation_hbm, innovation), (column_hbm, column), (nearby_hbm, nearby),
        ))
    ]
    for load in loads:
        load.start()

    barrier = pltpu.get_barrier_semaphore()

    def greet(semaphore, zz, xx, yy, cc):
        @pl.when((zz != z) | (xx != x) | (yy != y) | (cc != c))
        def _():
            pl.semaphore_signal(semaphore, inc=1, device_id=device(zz, xx, yy, cc), device_id_type=MESH)

    for j in range(8):
        greet(barrier, 2 * j + c, x, y, half)
        greet(barrier, 8 * c + j, x, y, parity)
        greet(barrier, z, j // 2, y, j % 2)
        greet(barrier, z_next, j // 2, y_next, j % 2)
        greet(barrier, z_prev, j // 2, y_prev, j % 2)
    self_obs = holder & (parity == c)
    def by_block(source, target):
        for j in range(source.shape[2] // 128):
            lanes = slice(128 * j, 128 * j + 128)
            for k in range(8):
                wide[pl.ds(1024 * j + k, 128, stride=8), :] = source[k, :, lanes].astype(F32)
            target[..., lanes] = wide[1024 * j : 1024 * j + 1024, :].astype(BF16).reshape(target.shape[:-1] + (128,))

    loads[0].wait()
    by_block(observed, obs)
    pl.semaphore_wait(barrier, 39 - 2 * self_obs.astype(jnp.int32))

    for j in range(8):
        greet(row_ready, 2 * j + c, x, y, half)

    def send_obs(t, carry):
        ii = lax.rem(inner + t, 8)
        zz = 8 * c + ii
        src = obs.at[pl.ds(pl.multiple_of(ii * 128, 128), 128)]
        pass_on(src, own_obs.at[lax.div(z, 2)], obs_send, obs_recv, device(zz, x, y, parity),
                (zz == z) & (parity == c))
        return carry

    lax.fori_loop(0, 8, send_obs, 0)

    loads[1].wait()
    by_block(states, chunks)

    def send_states(piece, turns, per_z):
        cols = pl.ds(piece * WIDTH, WIDTH)

        def body(t, carry):
            zz = 8 * c + lax.rem(inner + lax.div(t, per_z), 8)
            turn = turns + lax.rem(t, per_z)
            xx = lax.rem(x + lax.div(turn, 2), NX)
            cc = lax.rem(c + turn, 2)
            src = chunks.at[lax.rem(zz, 8) * 8 + 2 * xx + cc, :, cols]
            pass_on(src, arrived.at[slot_of(z, x), :, cols], st_send, st_recv.at[piece], device(zz, xx, y, cc),
                    (zz == z) & (xx == x) & (cc == c))
            return carry

        lax.fori_loop(0, 8 * per_z, body, 0)

    pl.semaphore_wait(row_ready, 8 - self_obs.astype(jnp.int32))
    for piece in range(PIECES):
        send_states(piece, 0, 2)

    for load in loads[2:]:
        load.wait()
    for j in range(2):
        lanes = slice(128 * j, 128 * j + 128)
        meta[pl.ds(j, 128, stride=8), :] = precision[:, lanes]
        meta[pl.ds(2 + j, 128, stride=8), :] = innovation[:, lanes]
        meta[pl.ds(4 + j, 128, stride=8), :] = column[:, lanes].astype(F32)
    block = region * 128 + lax.broadcasted_iota(jnp.int32, (128, 128), 1)
    reach = lax.broadcasted_iota(jnp.int32, (128, 128), 0) - RADIUS
    listed = jnp.zeros((128, 128), F32)
    for q in range(3):
        offset = ((nearby[q : q + 1, :] - block + NBLK // 2) & (NBLK - 1)) - NBLK // 2
        listed = jnp.where(offset == reach, F32(1.0), listed)
    listed = listed.T
    meta[pl.ds(6, 128, stride=8), :] = listed
    meta[pl.ds(7, 128, stride=8), :] = jnp.zeros((128, 128), F32)

    @pl.when(holder)
    def _():
        start = pl.multiple_of(inner * 128, 128)
        own = meta.at[pl.ds(start, 128)]
        pltpu.make_async_copy(own, meta_win.at[pl.ds(64, 128)], meta_recv).start()
        remote(own, meta_win.at[pl.ds(64, 128)], meta_send, meta_recv, device(z, x, y, 1 - c))
        for cc in range(2):
            remote(meta.at[pl.ds(start, 64)], meta_win.at[pl.ds(192, 64)], meta_send, meta_recv,
                   device(z_prev, x, y_prev, cc))
            remote(meta.at[pl.ds(start + 64, 64)], meta_win.at[pl.ds(0, 64)], meta_send, meta_recv,
                   device(z_next, x, y_next, cc))

    @pl.when(self_obs)
    def _():
        drain(own_obs.at[pl.ds(0, 7)], obs_send)

    @pl.when(jnp.logical_not(self_obs))
    def _():
        drain(own_obs, obs_send)

    drain(own_obs, obs_recv)

    mine_at = pl.ds(pl.multiple_of(place * 8, 8), 8)
    for t in range(PAIRS):

        def send_pair(step, carry):
            u = lax.rem(place + step, 8)
            q = u + 2 - t
            target = device(
                lax.select(q < 0, z_prev, lax.select(q > 7, z_next, z)),
                lax.rem(lax.div(q + 8, 2), NX),
                lax.select(q < 0, y_prev, lax.select(q > 7, y_next, y)),
                lax.rem(q + 8, 2),
            )
            pass_on(own_obs.at[:, pl.ds(pl.multiple_of(u * 16, 16), 16)], window.at[t, mine_at],
                    win_send, win_recv.at[t], target, q == place)
            return carry

        lax.fori_loop(0, 8, send_pair, 0)

    for piece in range(PIECES):
        send_states(piece, 2, 6)
    drain(meta_win, meta_recv)

    def meta_of(row):
        return meta_win[pl.ds(pl.multiple_of(row * 8, 8), 8), :]

    listed_by = [meta_of(8 + 2 * place + b)[6:7] for b in range(2)]
    forcing = [jnp.zeros((16, K), F32) for _ in range(2)]
    for t in range(PAIRS):
        drain(window.at[t], win_recv.at[t])
        rows = window[t].astype(F32)
        perts, innov = [], []
        for e in range(2):
            w = 2 * t + e
            about = meta_of(2 * place + 4 + w)
            innov.append(split_rows(as_row(about[2:4])))
            values = rows[:, 8 * e : 8 * e + 8, :].reshape(K, OBS)
            pert = (values - jnp.mean(values, axis=0, keepdims=True)).astype(BF16)
            perts.append(pert)
            for b in range(2):
                if 0 <= w - b <= 2 * RADIUS:
                    distance = F32(COLS * (w - b - RADIUS)) + about[4:6] - F32(0.5 * (COLS - 1))
                    decay = jnp.exp(-0.5 * jnp.square(distance / (0.5 * COLS * RADIUS)))
                    local = as_row(about[0:2] * decay * listed_by[b][:, w - b : w - b + 1])
                    weighted[b, e] = (pert.astype(F32) * local).astype(BF16)
        for b in range(2):
            for e in range(2):
                w = 2 * t + e
                if 0 <= w - b <= 2 * RADIUS:
                    term = dot_nt(perts[e], weighted[b, e])
                    full[b] = term if w == b else full[b] + term
                    forcing[b] = forcing[b] + dot_nt(innov[e], weighted[b, e])

    def put(b, k, rows, value):
        top = value.astype(BF16)
        high[b, k, rows, :] = top
        low[b, k, rows, :] = (value - top.astype(F32)).astype(BF16)

    def held(b, k, rows):
        return high[b, k, rows, :].astype(F32) + low[b, k, rows, :].astype(F32)

    def product(b, i, j, rows):
        left = high[b, i, rows, :]
        return dot_nn(left, high[b, j]) + dot_nn(left, low[b, j]) + dot_nn(low[b, i, rows, :], high[b, j])

    def tiles(step):
        @pl.loop(0, K // TILE)
        def _(t):
            start = pl.multiple_of(t * TILE, TILE)
            for b in range(2):
                step(b, pl.ds(start, TILE), start)

    def times(v, b, k):
        parts = split_rows(v)
        return jnp.sum(dot_nn(parts, high[b, k]) + dot_nn(parts, low[b, k]), axis=0, keepdims=True)

    R, F0, R1, M, Q, T, G, Z = range(8)
    inverse = []
    for b in range(2):
        diagonal = jnp.where(
            lax.broadcasted_iota(jnp.int32, (K, K), 0) == lax.broadcasted_iota(jnp.int32, (K, K), 1),
            F32(K - 1.0), F32(0.0))
        system = full[b] + diagonal
        full[b] = system
        sums = jnp.sum(jnp.abs(system), axis=0, keepdims=True)
        inverse.append(1.0 / jnp.max(sums, axis=1, keepdims=True))

    def scaled(b, rows, start):
        value = full[b, rows, :] * inverse[b]
        put(b, R, rows, value)
        put(b, F0, rows, identity_rows(start, 1.5) - 0.5 * value)

    def first(b, rows, start):
        put(b, R1, rows, 1.5 * full[b, rows, :] * inverse[b] - 0.5 * product(b, R, R, rows))

    def second(b, rows, start):
        put(b, M, rows, product(b, F0, R1, rows))

    def third(b, rows, start):
        value = product(b, M, M, rows)
        put(b, Q, rows, value)
        put(b, T, rows, identity_rows(start, 1.6875) - 0.5625 * held(b, M, rows) + 0.0625 * value)

    def fourth(b, rows, start):
        put(b, G, rows, identity_rows(start, 2.25) - 2.4375 * held(b, M, rows) + product(b, Q, T, rows))

    def fifth(b, rows, start):
        value = product(b, G, F0, rows)
        full[b, rows, :] = value
        put(b, Z, rows, value)

    for step in (scaled, first, second, third, fourth, fifth):
        tiles(step)

    mean_weight = [
        times(times(jnp.sum(forcing[b], axis=0, keepdims=True), b, Z), b, Z) * inverse[b] for b in range(2)
    ]
    scale = [jnp.sqrt((K - 1.0) * inverse[b]) for b in range(2)]

    def weights(b, rows, start):
        trans[b, rows, :] = (scale[b] * full[b, rows, :] + mean_weight[b]).astype(BF16)

    tiles(weights)

    for piece in range(PIECES):
        cols = pl.ds(piece * WIDTH, WIDTH)
        drain(arrived.at[:, :, cols], st_recv.at[piece])
        chunk = arrived[:, :, piece * WIDTH : (piece + 1) * WIDTH].astype(F32)
        blocks = []
        for b in range(2):
            values = chunk[:, 8 * b : 8 * b + 8, :].reshape(K, WIDTH)
            mean = jnp.mean(values, axis=0, keepdims=True)
            analysed = mean + dot_nn(trans[b], (values - mean).astype(BF16))
            blocks.append(analysed.reshape(64, 8, WIDTH))
        results[:, :, piece * WIDTH : (piece + 1) * WIDTH] = jnp.concatenate(blocks, axis=1).astype(BF16)

        def give_back(t, carry):
            step = lax.div(t, NX)
            zz = lax.rem(inner + step, 8) + 8 * lax.div(step, 8)
            xx = lax.rem(x + t, NX)
            pass_on(results.at[slot_of(zz, xx), :, cols], out.at[inner * 8 + place, :, cols], out_send, out_recv,
                    device(zz, xx, y, half), (zz == z) & (xx == x) & holder)
            return carry

        lax.fori_loop(0, 64, give_back, 0)

    drain(out, out_recv)

    @pl.when(holder)
    def _():
        drain(meta.at[pl.ds(0, 384)], meta_send)
        drain(chunks.at[pl.ds(0, 63)], st_send)
        drain(results.at[pl.ds(0, 63)], out_send)

    @pl.when(jnp.logical_not(holder))
    def _():
        drain(chunks, st_send)
        drain(results, out_send)

    for q in range(8):
        kept = sum(0 <= q + t - 2 <= 7 for t in range(PAIRS))

        @pl.when(place == q)
        def _():
            drain(own_obs.at[:, pl.ds(0, (8 - kept) * 16)], win_send)

    for _ in range(4):
        drain(own_obs, win_send)


def on_device(states, observed, precision, innovation, column, nearby):
    vmem = pl.BlockSpec(memory_space=pltpu.VMEM)
    dma = pltpu.SemaphoreType.DMA
    gathered = pl.pallas_call(
        kernel,
        out_shape=jax.ShapeDtypeStruct((64, 16, SITES), BF16),
        in_specs=[pl.BlockSpec(memory_space=pltpu.HBM)] * 6,
        out_specs=pl.BlockSpec(memory_space=pltpu.HBM),
        scratch_shapes=[
            pltpu.VMEM((8, 128, SITES), BF16),
            pltpu.VMEM((8, 128, OBS), BF16),
            pltpu.VMEM((128, OBS), F32),
            pltpu.VMEM((128, OBS), F32),
            pltpu.VMEM((128, OBS), jnp.int32),
            pltpu.VMEM((3, 128), jnp.int32),
            dma((6,)),
            pltpu.VMEM((SITES // 128 * 1024, 128), F32),
            pltpu.VMEM((64, 16, SITES), BF16),
            pltpu.VMEM((1024, OBS), BF16),
            pltpu.VMEM((1024, 128), F32),
            pltpu.VMEM((8, 128, OBS), BF16),
            pltpu.VMEM((PAIRS, 64, 16, OBS), BF16),
            pltpu.VMEM((64, 16, SITES), BF16),
            pltpu.VMEM((64, 16, SITES), BF16),
            pltpu.VMEM((256, 128), F32),
            pltpu.VMEM((2, 2, K, OBS), BF16),
            pltpu.VMEM((2, 8, K, K), BF16),
            pltpu.VMEM((2, 8, K, K), BF16),
            pltpu.VMEM((2, K, K), F32),
            pltpu.VMEM((2, K, K), BF16),
            dma, dma, dma, dma, dma, dma((PAIRS,)), dma, dma((PIECES,)), dma, dma, pltpu.SemaphoreType.REGULAR,
        ],
        compiler_params=pltpu.CompilerParams(
            collective_id=0, has_side_effects=True, vmem_limit_bytes=56 * 1024 * 1024
        ),
    )(states, observed, precision, innovation, column, nearby.T)
    return gathered.reshape(64, 2, 8, SITES).transpose(2, 0, 1, 3).reshape(8, 128, SITES)


def solution(mesh):
    split = P("region", None)
    placed = (P("member", "region", None), P("member", "region", None), split, split, split, split)
    return jax.shard_map(
        on_device, mesh=mesh, in_specs=placed, out_specs=P("member", "region", None), check_vma=False
    )
```

```python
import jax
import jax.numpy as jnp
from jax import lax
from jax.experimental import pallas as pl
from jax.experimental.pallas import tpu as pltpu
from jax.sharding import PartitionSpec as P

MESH = pl.DeviceIdType.MESH
F32 = jnp.float32
BF16 = jnp.bfloat16

COLS = 64
RADIUS = 4
NBLK = 1024
NZ, NX, NY = 16, 4, 4
K = 512
OBS = 256
SITES = 768
PAIRS = 5
PIECES = 3
WIDTH = SITES // PIECES
TILE = 256


def dot_nn(a, b):
    return jnp.dot(a, b, preferred_element_type=F32)


def dot_nt(a, b):
    return lax.dot_general(a, b, (((1,), (1,)), ((), ())), preferred_element_type=F32)


def split_rows(v):
    top = v.astype(BF16).astype(F32)
    rest = v - top
    mid = rest.astype(BF16).astype(F32)
    row = lax.broadcasted_iota(jnp.int32, (16, v.shape[1]), 0)
    zero = jnp.zeros((16, v.shape[1]), F32)
    stacked = jnp.where(row == 0, top, jnp.where(row == 1, mid, jnp.where(row == 2, rest - mid, zero)))
    return stacked.astype(BF16)


def as_row(v):
    return jnp.concatenate([v[0:1], v[1:2]], axis=1)


def identity_rows(start, scale):
    row = lax.broadcasted_iota(jnp.int32, (TILE, K), 0) + start
    col = lax.broadcasted_iota(jnp.int32, (TILE, K), 1)
    return jnp.where(row == col, F32(scale), F32(0.0))


def kernel(
    states_hbm, observed_hbm, precision_hbm, innovation_hbm, column_hbm, nearby_hbm, out,
    states, observed, precision, innovation, column, nearby, load_sem,
    wide, chunks, obs, meta, own_obs, window, arrived, results, meta_win, weighted, high, low, full, trans,
    meta_send, meta_recv, obs_send, obs_recv, win_send, win_recv, st_send, st_recv, out_send, out_recv,
    row_ready,
):
    member = lax.axis_index("member")
    region = lax.axis_index("region")
    z, x = lax.div(member, NX), lax.rem(member, NX)
    y, c = lax.div(region, 2), lax.rem(region, 2)
    half, inner = lax.div(z, 8), lax.rem(z, 8)
    place = 2 * x + c
    parity = lax.rem(z, 2)
    z_next, z_prev = lax.rem(z + 1, NZ), lax.rem(z + NZ - 1, NZ)
    y_next = lax.rem(y + lax.div(z + 1, NZ), NY)
    y_prev = lax.rem(y + NY - 1 + lax.div(z + NZ - 1, NZ), NY)
    holder = c == half

    def device(zz, xx, yy, cc):
        return (zz * NX + xx, yy * 2 + cc)

    def remote(src, dst, send, recv, target):
        pltpu.make_async_remote_copy(
            src_ref=src, dst_ref=dst, send_sem=send, recv_sem=recv, device_id=target, device_id_type=MESH
        ).start()

    def pass_on(src, dst, send, recv, target, mine):
        @pl.when(mine)
        def _():
            pltpu.make_async_copy(src, dst, recv).start()

        @pl.when(jnp.logical_not(mine))
        def _():
            remote(src, dst, send, recv, target)

    def drain(ref, sem):
        pltpu.make_async_copy(ref, ref, sem).wait()

    def slot_of(zz, xx):
        return xx * 16 + lax.rem(zz, 2) * 8 + lax.div(zz, 2)

    loads = [
        pltpu.make_async_copy(source, target, load_sem.at[k])
        for k, (source, target) in enumerate((
            (observed_hbm, observed), (states_hbm, states), (precision_hbm, precision),
            (innovation_hbm, innovation), (column_hbm, column), (nearby_hbm, nearby),
        ))
    ]
    for load in loads:
        load.start()

    barrier = pltpu.get_barrier_semaphore()

    def greet(semaphore, zz, xx, yy, cc):
        @pl.when((zz != z) | (xx != x) | (yy != y) | (cc != c))
        def _():
            pl.semaphore_signal(semaphore, inc=1, device_id=device(zz, xx, yy, cc), device_id_type=MESH)

    for j in range(8):
        greet(barrier, 2 * j + c, x, y, half)
        greet(barrier, 8 * c + j, x, y, parity)
        greet(barrier, z, j // 2, y, j % 2)
        greet(barrier, z_next, j // 2, y_next, j % 2)
        greet(barrier, z_prev, j // 2, y_prev, j % 2)
    self_obs = holder & (parity == c)
    def by_block(source, target):
        for j in range(source.shape[2] // 128):
            lanes = slice(128 * j, 128 * j + 128)
            for k in range(8):
                wide[pl.ds(1024 * j + k, 128, stride=8), :] = source[k, :, lanes].astype(F32)
            target[..., lanes] = wide[1024 * j : 1024 * j + 1024, :].astype(BF16).reshape(target.shape[:-1] + (128,))

    loads[0].wait()
    by_block(observed, obs)
    pl.semaphore_wait(barrier, 39 - 2 * self_obs.astype(jnp.int32))


    def send_obs(t, carry):
        ii = lax.rem(inner + t, 8)
        zz = 8 * c + ii
        src = obs.at[pl.ds(pl.multiple_of(ii * 128, 128), 128)]
        pass_on(src, own_obs.at[lax.div(z, 2)], obs_send, obs_recv, device(zz, x, y, parity),
                (zz == z) & (parity == c))
        return carry

    lax.fori_loop(0, 8, send_obs, 0)

    for j in range(8):
        greet(row_ready, 2 * j + c, x, y, half)

    loads[1].wait()
    by_block(states, chunks)

    def send_states(piece, turns, per_z):
        cols = pl.ds(piece * WIDTH, WIDTH)

        def body(t, carry):
            zz = 8 * c + lax.rem(inner + lax.div(t, per_z), 8)
            turn = turns + lax.rem(t, per_z)
            xx = lax.rem(x + lax.div(turn, 2), NX)
            cc = lax.rem(c + turn, 2)
            src = chunks.at[lax.rem(zz, 8) * 8 + 2 * xx + cc, :, cols]
            pass_on(src, arrived.at[slot_of(z, x), :, cols], st_send, st_recv.at[piece], device(zz, xx, y, cc),
                    (zz == z) & (xx == x) & (cc == c))
            return carry

        lax.fori_loop(0, 8 * per_z, body, 0)

    pl.semaphore_wait(row_ready, 8 - self_obs.astype(jnp.int32))
    for piece in range(PIECES):
        send_states(piece, 0, 2)

    for load in loads[2:]:
        load.wait()
    for j in range(2):
        lanes = slice(128 * j, 128 * j + 128)
        meta[pl.ds(j, 128, stride=8), :] = precision[:, lanes]
        meta[pl.ds(2 + j, 128, stride=8), :] = innovation[:, lanes]
        meta[pl.ds(4 + j, 128, stride=8), :] = column[:, lanes].astype(F32)
    block = region * 128 + lax.broadcasted_iota(jnp.int32, (128, 128), 1)
    reach = lax.broadcasted_iota(jnp.int32, (128, 128), 0) - RADIUS
    listed = jnp.zeros((128, 128), F32)
    for q in range(3):
        offset = ((nearby[q : q + 1, :] - block + NBLK // 2) & (NBLK - 1)) - NBLK // 2
        listed = jnp.where(offset == reach, F32(1.0), listed)
    listed = listed.T
    meta[pl.ds(6, 128, stride=8), :] = listed
    meta[pl.ds(7, 128, stride=8), :] = jnp.zeros((128, 128), F32)

    @pl.when(holder)
    def _():
        start = pl.multiple_of(inner * 128, 128)
        own = meta.at[pl.ds(start, 128)]
        pltpu.make_async_copy(own, meta_win.at[pl.ds(64, 128)], meta_recv).start()
        remote(own, meta_win.at[pl.ds(64, 128)], meta_send, meta_recv, device(z, x, y, 1 - c))
        for cc in range(2):
            remote(meta.at[pl.ds(start, 64)], meta_win.at[pl.ds(192, 64)], meta_send, meta_recv,
                   device(z_prev, x, y_prev, cc))
            remote(meta.at[pl.ds(start + 64, 64)], meta_win.at[pl.ds(0, 64)], meta_send, meta_recv,
                   device(z_next, x, y_next, cc))

    @pl.when(self_obs)
    def _():
        drain(own_obs.at[pl.ds(0, 7)], obs_send)

    @pl.when(jnp.logical_not(self_obs))
    def _():
        drain(own_obs, obs_send)

    drain(own_obs, obs_recv)

    mine_at = pl.ds(pl.multiple_of(place * 8, 8), 8)
    for t in range(PAIRS):

        def send_pair(step, carry):
            u = lax.rem(place + step, 8)
            q = u + 2 - t
            target = device(
                lax.select(q < 0, z_prev, lax.select(q > 7, z_next, z)),
                lax.rem(lax.div(q + 8, 2), NX),
                lax.select(q < 0, y_prev, lax.select(q > 7, y_next, y)),
                lax.rem(q + 8, 2),
            )
            pass_on(own_obs.at[:, pl.ds(pl.multiple_of(u * 16, 16), 16)], window.at[t, mine_at],
                    win_send, win_recv.at[t], target, q == place)
            return carry

        lax.fori_loop(0, 8, send_pair, 0)

    for piece in range(PIECES):
        send_states(piece, 2, 6)
    drain(meta_win, meta_recv)

    def meta_of(row):
        return meta_win[pl.ds(pl.multiple_of(row * 8, 8), 8), :]

    listed_by = [meta_of(8 + 2 * place + b)[6:7] for b in range(2)]
    forcing = [jnp.zeros((16, K), F32) for _ in range(2)]
    for t in range(PAIRS):
        drain(window.at[t], win_recv.at[t])
        rows = window[t].astype(F32)
        perts, innov = [], []
        for e in range(2):
            w = 2 * t + e
            about = meta_of(2 * place + 4 + w)
            innov.append(split_rows(as_row(about[2:4])))
            values = rows[:, 8 * e : 8 * e + 8, :].reshape(K, OBS)
            pert = (values - jnp.mean(values, axis=0, keepdims=True)).astype(BF16)
            perts.append(pert)
            for b in range(2):
                if 0 <= w - b <= 2 * RADIUS:
                    distance = F32(COLS * (w - b - RADIUS)) + about[4:6] - F32(0.5 * (COLS - 1))
                    decay = jnp.exp(-0.5 * jnp.square(distance / (0.5 * COLS * RADIUS)))
                    local = as_row(about[0:2] * decay * listed_by[b][:, w - b : w - b + 1])
                    weighted[b, e] = (pert.astype(F32) * local).astype(BF16)
        for b in range(2):
            for e in range(2):
                w = 2 * t + e
                if 0 <= w - b <= 2 * RADIUS:
                    term = dot_nt(perts[e], weighted[b, e])
                    full[b] = term if w == b else full[b] + term
                    forcing[b] = forcing[b] + dot_nt(innov[e], weighted[b, e])

    def put(b, k, rows, value):
        top = value.astype(BF16)
        high[b, k, rows, :] = top
        low[b, k, rows, :] = (value - top.astype(F32)).astype(BF16)

    def held(b, k, rows):
        return high[b, k, rows, :].astype(F32) + low[b, k, rows, :].astype(F32)

    def product(b, i, j, rows):
        left = high[b, i, rows, :]
        return dot_nn(left, high[b, j]) + dot_nn(left, low[b, j]) + dot_nn(low[b, i, rows, :], high[b, j])

    def tiles(step):
        @pl.loop(0, K // TILE)
        def _(t):
            start = pl.multiple_of(t * TILE, TILE)
            for b in range(2):
                step(b, pl.ds(start, TILE), start)

    def times(v, b, k):
        parts = split_rows(v)
        return jnp.sum(dot_nn(parts, high[b, k]) + dot_nn(parts, low[b, k]), axis=0, keepdims=True)

    R, F0, R1, M, Q, T, G, Z = range(8)
    inverse = []
    for b in range(2):
        diagonal = jnp.where(
            lax.broadcasted_iota(jnp.int32, (K, K), 0) == lax.broadcasted_iota(jnp.int32, (K, K), 1),
            F32(K - 1.0), F32(0.0))
        system = full[b] + diagonal
        full[b] = system
        sums = jnp.sum(jnp.abs(system), axis=0, keepdims=True)
        inverse.append(1.0 / jnp.max(sums, axis=1, keepdims=True))

    def scaled(b, rows, start):
        value = full[b, rows, :] * inverse[b]
        put(b, R, rows, value)
        put(b, F0, rows, identity_rows(start, 1.5) - 0.5 * value)

    def first(b, rows, start):
        put(b, R1, rows, 1.5 * full[b, rows, :] * inverse[b] - 0.5 * product(b, R, R, rows))

    def second(b, rows, start):
        put(b, M, rows, product(b, F0, R1, rows))

    def third(b, rows, start):
        value = product(b, M, M, rows)
        put(b, Q, rows, value)
        put(b, T, rows, identity_rows(start, 1.6875) - 0.5625 * held(b, M, rows) + 0.0625 * value)

    def fourth(b, rows, start):
        put(b, G, rows, identity_rows(start, 2.25) - 2.4375 * held(b, M, rows) + product(b, Q, T, rows))

    def fifth(b, rows, start):
        value = product(b, G, F0, rows)
        full[b, rows, :] = value
        put(b, Z, rows, value)

    for step in (scaled, first, second, third, fourth, fifth):
        tiles(step)

    mean_weight = [
        times(times(jnp.sum(forcing[b], axis=0, keepdims=True), b, Z), b, Z) * inverse[b] for b in range(2)
    ]
    scale = [jnp.sqrt((K - 1.0) * inverse[b]) for b in range(2)]

    def weights(b, rows, start):
        trans[b, rows, :] = (scale[b] * full[b, rows, :] + mean_weight[b]).astype(BF16)

    tiles(weights)

    for piece in range(PIECES):
        cols = pl.ds(piece * WIDTH, WIDTH)
        drain(arrived.at[:, :, cols], st_recv.at[piece])
        chunk = arrived[:, :, piece * WIDTH : (piece + 1) * WIDTH].astype(F32)
        blocks = []
        for b in range(2):
            values = chunk[:, 8 * b : 8 * b + 8, :].reshape(K, WIDTH)
            mean = jnp.mean(values, axis=0, keepdims=True)
            analysed = mean + dot_nn(trans[b], (values - mean).astype(BF16))
            blocks.append(analysed.reshape(64, 8, WIDTH))
        results[:, :, piece * WIDTH : (piece + 1) * WIDTH] = jnp.concatenate(blocks, axis=1).astype(BF16)

        def give_back(t, carry):
            step = lax.div(t, NX)
            zz = lax.rem(inner + step, 8) + 8 * lax.div(step, 8)
            xx = lax.rem(x + t, NX)
            pass_on(results.at[slot_of(zz, xx), :, cols], out.at[inner * 8 + place, :, cols], out_send, out_recv,
                    device(zz, xx, y, half), (zz == z) & (xx == x) & holder)
            return carry

        lax.fori_loop(0, 64, give_back, 0)

    drain(out, out_recv)

    @pl.when(holder)
    def _():
        drain(meta.at[pl.ds(0, 384)], meta_send)
        drain(chunks.at[pl.ds(0, 63)], st_send)
        drain(results.at[pl.ds(0, 63)], out_send)

    @pl.when(jnp.logical_not(holder))
    def _():
        drain(chunks, st_send)
        drain(results, out_send)

    for q in range(8):
        kept = sum(0 <= q + t - 2 <= 7 for t in range(PAIRS))

        @pl.when(place == q)
        def _():
            drain(own_obs.at[:, pl.ds(0, (8 - kept) * 16)], win_send)

    for _ in range(4):
        drain(own_obs, win_send)


def on_device(states, observed, precision, innovation, column, nearby):
    vmem = pl.BlockSpec(memory_space=pltpu.VMEM)
    dma = pltpu.SemaphoreType.DMA
    gathered = pl.pallas_call(
        kernel,
        out_shape=jax.ShapeDtypeStruct((64, 16, SITES), BF16),
        in_specs=[pl.BlockSpec(memory_space=pltpu.HBM)] * 6,
        out_specs=vmem,
        scratch_shapes=[
            pltpu.VMEM((8, 128, SITES), BF16),
            pltpu.VMEM((8, 128, OBS), BF16),
            pltpu.VMEM((128, OBS), F32),
            pltpu.VMEM((128, OBS), F32),
            pltpu.VMEM((128, OBS), jnp.int32),
            pltpu.VMEM((3, 128), jnp.int32),
            dma((6,)),
            pltpu.VMEM((SITES // 128 * 1024, 128), F32),
            pltpu.VMEM((64, 16, SITES), BF16),
            pltpu.VMEM((1024, OBS), BF16),
            pltpu.VMEM((1024, 128), F32),
            pltpu.VMEM((8, 128, OBS), BF16),
            pltpu.VMEM((PAIRS, 64, 16, OBS), BF16),
            pltpu.VMEM((64, 16, SITES), BF16),
            pltpu.VMEM((64, 16, SITES), BF16),
            pltpu.VMEM((256, 128), F32),
            pltpu.VMEM((2, 2, K, OBS), BF16),
            pltpu.VMEM((2, 8, K, K), BF16),
            pltpu.VMEM((2, 8, K, K), BF16),
            pltpu.VMEM((2, K, K), F32),
            pltpu.VMEM((2, K, K), BF16),
            dma, dma, dma, dma, dma, dma((PAIRS,)), dma, dma((PIECES,)), dma, dma, pltpu.SemaphoreType.REGULAR,
        ],
        compiler_params=pltpu.CompilerParams(
            collective_id=0, has_side_effects=True, vmem_limit_bytes=44 * 1024 * 1024
        ),
    )(*(pltpu.with_memory_space_constraint(a, pltpu.HBM)
        for a in (states, observed, precision, innovation, column, nearby.T)))
    return gathered.reshape(64, 2, 8, SITES).transpose(2, 0, 1, 3).reshape(8, 128, SITES)


def solution(mesh):
    split = P("region", None)
    placed = (P("member", "region", None), P("member", "region", None), split, split, split, split)
    return jax.shard_map(
        on_device, mesh=mesh, in_specs=placed, out_specs=P("member", "region", None), check_vma=False
    )
```

```python
import jax
import jax.numpy as jnp
from jax import lax
from jax.experimental import pallas as pl
from jax.experimental.pallas import tpu as pltpu
from jax.sharding import PartitionSpec as P

MESH = pl.DeviceIdType.MESH
F32 = jnp.float32
BF16 = jnp.bfloat16

COLS = 64
RADIUS = 4
NBLK = 1024
NZ, NX, NY = 16, 4, 4
K = 512
OBS = 256
SITES = 768
PAIRS = 5
PIECES = 3
WIDTH = SITES // PIECES
TILE = 256


def dot_nn(a, b):
    return jnp.dot(a, b, preferred_element_type=F32)


def dot_nt(a, b):
    return lax.dot_general(a, b, (((1,), (1,)), ((), ())), preferred_element_type=F32)


def split_rows(v):
    top = v.astype(BF16).astype(F32)
    rest = v - top
    mid = rest.astype(BF16).astype(F32)
    row = lax.broadcasted_iota(jnp.int32, (16, v.shape[1]), 0)
    zero = jnp.zeros((16, v.shape[1]), F32)
    stacked = jnp.where(row == 0, top, jnp.where(row == 1, mid, jnp.where(row == 2, rest - mid, zero)))
    return stacked.astype(BF16)


def as_row(v):
    return jnp.concatenate([v[0:1], v[1:2]], axis=1)


def identity_rows(start, scale):
    row = lax.broadcasted_iota(jnp.int32, (TILE, K), 0) + start
    col = lax.broadcasted_iota(jnp.int32, (TILE, K), 1)
    return jnp.where(row == col, F32(scale), F32(0.0))


def kernel(
    states_hbm, observed_hbm, precision_hbm, innovation_hbm, column_hbm, nearby_hbm, out,
    states, observed, precision, innovation, column, nearby, load_sem,
    wide, chunks, obs, meta, own_obs, window, arrived, results, meta_win, weighted, high, low, full, trans,
    meta_send, meta_recv, obs_send, obs_recv, win_send, win_recv, st_send, st_recv, out_send, out_recv,
    row_ready, end_send,
):
    member = lax.axis_index("member")
    region = lax.axis_index("region")
    z, x = lax.div(member, NX), lax.rem(member, NX)
    y, c = lax.div(region, 2), lax.rem(region, 2)
    half, inner = lax.div(z, 8), lax.rem(z, 8)
    place = 2 * x + c
    parity = lax.rem(z, 2)
    z_next, z_prev = lax.rem(z + 1, NZ), lax.rem(z + NZ - 1, NZ)
    y_next = lax.rem(y + lax.div(z + 1, NZ), NY)
    y_prev = lax.rem(y + NY - 1 + lax.div(z + NZ - 1, NZ), NY)
    holder = c == half

    def device(zz, xx, yy, cc):
        return (zz * NX + xx, yy * 2 + cc)

    def remote(src, dst, send, recv, target):
        pltpu.make_async_remote_copy(
            src_ref=src, dst_ref=dst, send_sem=send, recv_sem=recv, device_id=target, device_id_type=MESH
        ).start()

    def pass_on(src, dst, send, recv, target, mine):
        @pl.when(mine)
        def _():
            pltpu.make_async_copy(src, dst, recv).start()

        @pl.when(jnp.logical_not(mine))
        def _():
            remote(src, dst, send, recv, target)

    def drain(ref, sem):
        pltpu.make_async_copy(ref, ref, sem).wait()

    def slot_of(zz, xx):
        return xx * 16 + lax.rem(zz, 2) * 8 + lax.div(zz, 2)

    loads = [
        pltpu.make_async_copy(source, target, load_sem.at[k])
        for k, (source, target) in enumerate((
            (observed_hbm, observed), (states_hbm, states), (precision_hbm, precision),
            (innovation_hbm, innovation), (column_hbm, column), (nearby_hbm, nearby),
        ))
    ]
    for load in loads:
        load.start()

    barrier = pltpu.get_barrier_semaphore()

    def greet(semaphore, zz, xx, yy, cc):
        @pl.when((zz != z) | (xx != x) | (yy != y) | (cc != c))
        def _():
            pl.semaphore_signal(semaphore, inc=1, device_id=device(zz, xx, yy, cc), device_id_type=MESH)

    for j in range(8):
        greet(barrier, 2 * j + c, x, y, half)
        greet(barrier, 8 * c + j, x, y, parity)
        greet(barrier, z, j // 2, y, j % 2)
        greet(barrier, z_next, j // 2, y_next, j % 2)
        greet(barrier, z_prev, j // 2, y_prev, j % 2)
    self_obs = holder & (parity == c)
    def by_block(source, target):
        for j in range(source.shape[2] // 128):
            lanes = slice(128 * j, 128 * j + 128)
            for k in range(8):
                wide[pl.ds(1024 * j + k, 128, stride=8), :] = source[k, :, lanes].astype(F32)
            target[..., lanes] = wide[1024 * j : 1024 * j + 1024, :].astype(BF16).reshape(target.shape[:-1] + (128,))

    loads[0].wait()
    by_block(observed, obs)
    pl.semaphore_wait(barrier, 39 - 2 * self_obs.astype(jnp.int32))


    def send_obs(t, carry):
        ii = lax.rem(inner + t, 8)
        zz = 8 * c + ii
        src = obs.at[pl.ds(pl.multiple_of(ii * 128, 128), 128)]
        pass_on(src, own_obs.at[lax.div(z, 2)], obs_send, obs_recv, device(zz, x, y, parity),
                (zz == z) & (parity == c))
        return carry

    lax.fori_loop(0, 8, send_obs, 0)

    for j in range(8):
        greet(row_ready, 2 * j + c, x, y, half)

    loads[1].wait()
    by_block(states, chunks)

    def send_states(piece, turns, per_z):
        cols = pl.ds(piece * WIDTH, WIDTH)

        def body(t, carry):
            zz = 8 * c + lax.rem(inner + lax.div(t, per_z), 8)
            turn = turns + lax.rem(t, per_z)
            xx = lax.rem(x + lax.div(turn, 2), NX)
            cc = lax.rem(c + turn, 2)
            src = chunks.at[lax.rem(zz, 8) * 8 + 2 * xx + cc, :, cols]
            pass_on(src, arrived.at[slot_of(z, x), :, cols], st_send, st_recv.at[piece], device(zz, xx, y, cc),
                    (zz == z) & (xx == x) & (cc == c))
            return carry

        lax.fori_loop(0, 8 * per_z, body, 0)

    pl.semaphore_wait(row_ready, 8 - self_obs.astype(jnp.int32))
    for piece in range(PIECES):
        send_states(piece, 0, 2)

    for load in loads[2:]:
        load.wait()
    for j in range(2):
        lanes = slice(128 * j, 128 * j + 128)
        meta[pl.ds(j, 128, stride=8), :] = precision[:, lanes]
        meta[pl.ds(2 + j, 128, stride=8), :] = innovation[:, lanes]
        meta[pl.ds(4 + j, 128, stride=8), :] = column[:, lanes].astype(F32)
    block = region * 128 + lax.broadcasted_iota(jnp.int32, (128, 128), 1)
    reach = lax.broadcasted_iota(jnp.int32, (128, 128), 0) - RADIUS
    listed = jnp.zeros((128, 128), F32)
    for q in range(3):
        offset = ((nearby[q : q + 1, :] - block + NBLK // 2) & (NBLK - 1)) - NBLK // 2
        listed = jnp.where(offset == reach, F32(1.0), listed)
    listed = listed.T
    meta[pl.ds(6, 128, stride=8), :] = listed
    meta[pl.ds(7, 128, stride=8), :] = jnp.zeros((128, 128), F32)

    @pl.when(holder)
    def _():
        start = pl.multiple_of(inner * 128, 128)
        own = meta.at[pl.ds(start, 128)]
        pltpu.make_async_copy(own, meta_win.at[pl.ds(64, 128)], meta_recv).start()
        remote(own, meta_win.at[pl.ds(64, 128)], meta_send, meta_recv, device(z, x, y, 1 - c))
        for cc in range(2):
            remote(meta.at[pl.ds(start, 64)], meta_win.at[pl.ds(192, 64)], meta_send, meta_recv,
                   device(z_prev, x, y_prev, cc))
            remote(meta.at[pl.ds(start + 64, 64)], meta_win.at[pl.ds(0, 64)], meta_send, meta_recv,
                   device(z_next, x, y_next, cc))

    @pl.when(self_obs)
    def _():
        drain(own_obs.at[pl.ds(0, 7)], obs_send)

    @pl.when(jnp.logical_not(self_obs))
    def _():
        drain(own_obs, obs_send)

    drain(own_obs, obs_recv)

    mine_at = pl.ds(pl.multiple_of(place * 8, 8), 8)
    for t in range(PAIRS):

        skipped = {0: 7, PAIRS - 1: 0}.get(t, -1)

        def send_pair(step, carry):
            u = lax.rem(place + step, 8)
            q = u + 2 - t
            target = device(
                lax.select(q < 0, z_prev, lax.select(q > 7, z_next, z)),
                lax.rem(lax.div(q + 8, 2), NX),
                lax.select(q < 0, y_prev, lax.select(q > 7, y_next, y)),
                lax.rem(q + 8, 2),
            )

            @pl.when(u != skipped)
            def _():
                pass_on(own_obs.at[:, pl.ds(pl.multiple_of(u * 16, 16), 16)], window.at[t, mine_at],
                        win_send, win_recv.at[t], target, q == place)

            return carry

        lax.fori_loop(0, 8, send_pair, 0)

    for piece in range(PIECES):
        send_states(piece, 2, 6)
    drain(meta_win, meta_recv)

    def meta_of(row):
        return meta_win[pl.ds(pl.multiple_of(row * 8, 8), 8), :]

    listed_by = [meta_of(8 + 2 * place + b)[6:7] for b in range(2)]
    forcing = [jnp.zeros((16, K), F32) for _ in range(2)]
    for end, came, goes in ((0, 1, 0), (7, 3, 4)):

        @pl.when(place == end)
        def _():
            drain(window.at[came], win_recv.at[came])
            remote(window.at[came], window.at[goes], end_send, win_recv.at[goes], device(z, x, y, 1 - c))

    for t in range(PAIRS):
        taken = ((place == 0) & (t == 1)) | ((place == 7) & (t == 3))

        @pl.when(jnp.logical_not(taken))
        def _():
            drain(window.at[t], win_recv.at[t])

        rows = window[t].astype(F32)
        perts, innov = [], []
        for e in range(2):
            w = 2 * t + e
            about = meta_of(2 * place + 4 + w)
            innov.append(split_rows(as_row(about[2:4])))
            values = rows[:, 8 * e : 8 * e + 8, :].reshape(K, OBS)
            pert = (values - jnp.mean(values, axis=0, keepdims=True)).astype(BF16)
            perts.append(pert)
            for b in range(2):
                if 0 <= w - b <= 2 * RADIUS:
                    distance = F32(COLS * (w - b - RADIUS)) + about[4:6] - F32(0.5 * (COLS - 1))
                    decay = jnp.exp(-0.5 * jnp.square(distance / (0.5 * COLS * RADIUS)))
                    local = as_row(about[0:2] * decay * listed_by[b][:, w - b : w - b + 1])
                    weighted[b, e] = (pert.astype(F32) * local).astype(BF16)
        for b in range(2):
            for e in range(2):
                w = 2 * t + e
                if 0 <= w - b <= 2 * RADIUS:
                    term = dot_nt(perts[e], weighted[b, e])
                    full[b] = term if w == b else full[b] + term
                    forcing[b] = forcing[b] + dot_nt(innov[e], weighted[b, e])

    def put(b, k, rows, value):
        top = value.astype(BF16)
        high[b, k, rows, :] = top
        low[b, k, rows, :] = (value - top.astype(F32)).astype(BF16)

    def held(b, k, rows):
        return high[b, k, rows, :].astype(F32) + low[b, k, rows, :].astype(F32)

    def product(b, i, j, rows):
        left = high[b, i, rows, :]
        return dot_nn(left, high[b, j]) + dot_nn(left, low[b, j]) + dot_nn(low[b, i, rows, :], high[b, j])

    def tiles(step):
        @pl.loop(0, K // TILE)
        def _(t):
            start = pl.multiple_of(t * TILE, TILE)
            for b in range(2):
                step(b, pl.ds(start, TILE), start)

    def times(v, b, k):
        parts = split_rows(v)
        return jnp.sum(dot_nn(parts, high[b, k]) + dot_nn(parts, low[b, k]), axis=0, keepdims=True)

    R, F0, R1, M, Q, T, G, Z = range(8)
    inverse = []
    for b in range(2):
        diagonal = jnp.where(
            lax.broadcasted_iota(jnp.int32, (K, K), 0) == lax.broadcasted_iota(jnp.int32, (K, K), 1),
            F32(K - 1.0), F32(0.0))
        system = full[b] + diagonal
        full[b] = system
        sums = jnp.sum(jnp.abs(system), axis=0, keepdims=True)
        inverse.append(1.0 / jnp.max(sums, axis=1, keepdims=True))

    def scaled(b, rows, start):
        value = full[b, rows, :] * inverse[b]
        put(b, R, rows, value)
        put(b, F0, rows, identity_rows(start, 1.5) - 0.5 * value)

    def first(b, rows, start):
        put(b, R1, rows, 1.5 * full[b, rows, :] * inverse[b] - 0.5 * product(b, R, R, rows))

    def second(b, rows, start):
        put(b, M, rows, product(b, F0, R1, rows))

    def third(b, rows, start):
        value = product(b, M, M, rows)
        put(b, Q, rows, value)
        put(b, T, rows, identity_rows(start, 1.6875) - 0.5625 * held(b, M, rows) + 0.0625 * value)

    def fourth(b, rows, start):
        put(b, G, rows, identity_rows(start, 2.25) - 2.4375 * held(b, M, rows) + product(b, Q, T, rows))

    def fifth(b, rows, start):
        value = product(b, G, F0, rows)
        full[b, rows, :] = value
        put(b, Z, rows, value)

    for step in (scaled, first, second, third, fourth, fifth):
        tiles(step)

    mean_weight = [
        times(times(jnp.sum(forcing[b], axis=0, keepdims=True), b, Z), b, Z) * inverse[b] for b in range(2)
    ]
    scale = [jnp.sqrt((K - 1.0) * inverse[b]) for b in range(2)]

    def weights(b, rows, start):
        trans[b, rows, :] = (scale[b] * full[b, rows, :] + mean_weight[b]).astype(BF16)

    tiles(weights)

    for piece in range(PIECES):
        cols = pl.ds(piece * WIDTH, WIDTH)
        drain(arrived.at[:, :, cols], st_recv.at[piece])
        chunk = arrived[:, :, piece * WIDTH : (piece + 1) * WIDTH].astype(F32)
        blocks = []
        for b in range(2):
            values = chunk[:, 8 * b : 8 * b + 8, :].reshape(K, WIDTH)
            mean = jnp.mean(values, axis=0, keepdims=True)
            analysed = mean + dot_nn(trans[b], (values - mean).astype(BF16))
            blocks.append(analysed.reshape(64, 8, WIDTH))
        results[:, :, piece * WIDTH : (piece + 1) * WIDTH] = jnp.concatenate(blocks, axis=1).astype(BF16)

        def give_back(t, carry):
            step = lax.div(t, NX)
            zz = lax.rem(inner + step, 8) + 8 * lax.div(step, 8)
            xx = lax.rem(x + t, NX)
            pass_on(results.at[slot_of(zz, xx), :, cols], out.at[inner * 8 + place, :, cols], out_send, out_recv,
                    device(zz, xx, y, half), (zz == z) & (xx == x) & holder)
            return carry

        lax.fori_loop(0, 64, give_back, 0)

    drain(out, out_recv)

    @pl.when(holder)
    def _():
        drain(meta.at[pl.ds(0, 384)], meta_send)
        drain(chunks.at[pl.ds(0, 63)], st_send)
        drain(results.at[pl.ds(0, 63)], out_send)

    @pl.when(jnp.logical_not(holder))
    def _():
        drain(chunks, st_send)
        drain(results, out_send)

    @pl.when((place == 0) | (place == 7))
    def _():
        drain(window.at[0], end_send)

    for q in range(8):
        kept = sum(0 <= q + t - 2 <= 7 for t in range(PAIRS))

        @pl.when(place == q)
        def _():
            drain(own_obs.at[:, pl.ds(0, (6 - kept) * 16)], win_send)

    for _ in range(4):
        drain(own_obs, win_send)


def on_device(states, observed, precision, innovation, column, nearby):
    vmem = pl.BlockSpec(memory_space=pltpu.VMEM)
    dma = pltpu.SemaphoreType.DMA
    gathered = pl.pallas_call(
        kernel,
        out_shape=jax.ShapeDtypeStruct((64, 16, SITES), BF16),
        in_specs=[pl.BlockSpec(memory_space=pltpu.HBM)] * 6,
        out_specs=vmem,
        scratch_shapes=[
            pltpu.VMEM((8, 128, SITES), BF16),
            pltpu.VMEM((8, 128, OBS), BF16),
            pltpu.VMEM((128, OBS), F32),
            pltpu.VMEM((128, OBS), F32),
            pltpu.VMEM((128, OBS), jnp.int32),
            pltpu.VMEM((3, 128), jnp.int32),
            dma((6,)),
            pltpu.VMEM((SITES // 128 * 1024, 128), F32),
            pltpu.VMEM((64, 16, SITES), BF16),
            pltpu.VMEM((1024, OBS), BF16),
            pltpu.VMEM((1024, 128), F32),
            pltpu.VMEM((8, 128, OBS), BF16),
            pltpu.VMEM((PAIRS, 64, 16, OBS), BF16),
            pltpu.VMEM((64, 16, SITES), BF16),
            pltpu.VMEM((64, 16, SITES), BF16),
            pltpu.VMEM((256, 128), F32),
            pltpu.VMEM((2, 2, K, OBS), BF16),
            pltpu.VMEM((2, 8, K, K), BF16),
            pltpu.VMEM((2, 8, K, K), BF16),
            pltpu.VMEM((2, K, K), F32),
            pltpu.VMEM((2, K, K), BF16),
            dma, dma, dma, dma, dma, dma((PAIRS,)), dma, dma((PIECES,)), dma, dma, pltpu.SemaphoreType.REGULAR, dma,
        ],
        compiler_params=pltpu.CompilerParams(
            collective_id=0, has_side_effects=True, vmem_limit_bytes=44 * 1024 * 1024
        ),
    )(*(pltpu.with_memory_space_constraint(a, pltpu.HBM)
        for a in (states, observed, precision, innovation, column, nearby.T)))
    return gathered.reshape(64, 2, 8, SITES).transpose(2, 0, 1, 3).reshape(8, 128, SITES)


def solution(mesh):
    split = P("region", None)
    placed = (P("member", "region", None), P("member", "region", None), split, split, split, split)
    return jax.shard_map(
        on_device, mesh=mesh, in_specs=placed, out_specs=P("member", "region", None), check_vma=False
    )
```
